32 devices in a mesh: groups: 2 (over y), expert: 4 (over z), replica: 4 (over x, core).
Axes of the slice: x: 2, y: 2, z: 4, core: 2. Of those that a mesh axis runs over, the one named last changes fastest.
Arguments:
- moe_rows: bfloat16 [128, 7168], P(('groups', 'expert', 'replica')), parts along dimension 0, may hold values from -6 to 6
- expert_ids: int32 [128, 8], P(('groups', 'expert', 'replica')), parts along dimension 0, may hold values from 0 to 31, all different within a row; in each aligned block of 4 rows (0 to 3, 4 to 7, ...) at most 2 rows name the same one
- expert_weights: float32 [128, 8], P(('groups', 'expert', 'replica')), parts along dimension 0, may hold values from 0.05 to 0.5
- w_gate: bfloat16 [32, 7168, 1024], P('expert', None, 'replica'), may hold values from -0.0625 to 0.0625
- w_up: bfloat16 [32, 7168, 1024], P('expert', None, 'replica'), may hold values from -0.0625 to 0.0625
- w_down: bfloat16 [32, 1024, 7168], P('expert', 'replica'), may hold values from -0.1875 to 0.1875
- queries: bfloat16 [128, 64, 576], P(('groups', 'expert', 'replica')), parts along dimension 0, may hold values from -120 to 120
- latent_cache: bfloat16 [128, 256, 576], P(('groups', 'expert', 'replica')), parts along dimension 0, may hold values from -4 to 4
- cache_lengths: int32 [128], P(('groups', 'expert', 'replica')), parts along dimension 0, may hold values from 2 to 256, as said below
- move_src: int32 [128], P(('groups', 'expert', 'replica')), parts along dimension 0, may hold values from 0 to 15, as said below
Outputs:
- moe_out: bfloat16 [128, 7168], P(('groups', 'expert', 'replica')), parts along dimension 0
- context: bfloat16 [128, 64, 512], P(('groups', 'expert', 'replica')), parts along dimension 0
The draws below stay inside these ranges and needn't reach their ends.
There are 2 independent parts, one for each index of `groups`. The reference program is written for one: setup_inputs(seed, part) draws one part's arguments, and reference() takes and returns one part's arrays. A program takes and returns all parts, laid end to end along the dimension named above; an argument that names none is the same for every part. Nothing has to cross between parts.
Inputs may be any that keep to these rules, and one draw needn't show every extreme that they name: `expert_ids`: each row names 8 different experts; within the rows of one device (aligned blocks of 4 rows) no expert is named more than 2 times, a bound that some block reaches. `move_src`: each aligned block of 16 entries is a permutation of 0 to 15. `cache_lengths`: some request holds exactly 256 positions.
All inputs are finite; a program needn't handle non-finite values.
Results may differ from the reference program's by a relative error of at most 0.0057.
Values may be sent and summed in bfloat16 or wider, within the bound.
A program may use at most 256 MiB of HBM per device.

```python
import math
import jax
import jax.numpy as jnp
import numpy as np
from jax import lax

D = 7168
FF = 1024
H = 64
LAT = 512
ROPE = 64
EXPERTS = 32
TOPK = 8
TOK_DEV = 4
L = 256
CAP = 2
TOKENS = 64
REQS = 64
GROUP_REQ = 16
N_EXPERT = 4
N_REPLICA = 4


def reassign(key):
    group_keys = jax.random.split(jax.random.fold_in(key, 11), REQS // GROUP_REQ)
    orders = jax.vmap(lambda single: jax.random.permutation(single, GROUP_REQ))(group_keys)
    return orders.reshape(-1).astype(jnp.int32)


def draw_move_src(key, part):
    return reassign(key)


def draw_latent_cache(key, part):
    salted = jax.random.fold_in(key, 3)
    values_base = jnp.clip(jax.random.normal(salted, (REQS, L, LAT + ROPE), jnp.float32), -4.0, 4.0)
    return values_base.astype(jnp.bfloat16)


def draw_cache_lengths(key, part):
    salted = jax.random.fold_in(key, 5)
    first_key, second_key = jax.random.split(salted, 2)
    lengths = jax.random.randint(first_key, (REQS,), 2, L + 1, dtype=jnp.int32)
    longest = jax.random.randint(second_key, (), 0, REQS, dtype=jnp.int32)
    return lengths.at[longest].set(L)


def draw_queries(key, part):
    salted = jax.random.fold_in(key, 7)
    first_key = jax.random.fold_in(salted, 0)
    values_base = jnp.clip(jax.random.normal(first_key, (REQS, H, LAT + ROPE), jnp.float32), -4.0, 4.0)
    return values_base.astype(jnp.bfloat16)


def block_levels(rng, dims, cuts, low, top_value):
    def one(axis_at, parts):
        draws = jax.random.uniform(jax.random.fold_in(jax.random.fold_in(rng, 6), axis_at), (parts,), jnp.float32, low / len(cuts), top_value / len(cuts))
        return jnp.repeat(jnp.exp(draws), dims[axis_at] // parts).reshape((-1,) + (1,) * (len(dims) - axis_at - 1))

    gain = one(*cuts[0])
    for cut in cuts[1:]:
        gain = gain * one(*cut)
    return gain


def deal_out(own_key, own, number, rows, number_of, top, reach, lean):
    sequence = jax.random.permutation(own_key, number_of)
    heavy_load, ordinary = load_shares(number_of, rows * top, reach, lean, True), load_shares(number_of, rows * top, reach, lean, False)
    places = jnp.arange(number_of)

    def named(sizes, rotation):
        used = int((sizes > 0).sum())
        fixed = max(1, used // 4)
        shifted = fixed + (places - fixed + rotation * (used - fixed)) % max(1, number_of - fixed)
        return jnp.zeros((number_of,), jnp.int32).at[sequence[jnp.where(places < fixed, places, shifted)]].set(jnp.asarray(sizes, jnp.int32))

    sizes = jnp.where(number % 4 == 0, named(heavy_load, number // 4), named(ordinary, number - number // 4 - 1))
    mixed = jax.random.permutation(jax.random.fold_in(own, 3), number_of)
    giver, taker = mixed[0:number_of // 2 * 2:2], mixed[1:number_of // 2 * 2:2]
    slack = jnp.minimum(sizes[giver] - 1, reach - sizes[taker]) // 2
    slack = jnp.where((giver == sequence[0]) | (taker == sequence[0]) | (sizes[taker] == 0), 0, jnp.maximum(slack, 0))
    shifted = jax.random.randint(jax.random.fold_in(own, 4), (number_of // 2,), 0, 1 << 20) % (slack + 1)
    sizes = sizes.at[giver].add(-shifted).at[taker].add(shifted)
    items = jnp.searchsorted(jnp.cumsum(sizes), jnp.arange(rows * top), side="right").astype(jnp.int32)
    table = items.reshape(top, rows).T
    table = table[jax.random.permutation(jax.random.fold_in(own, 1), rows)]
    rotation = jax.random.randint(jax.random.fold_in(own, 2), (rows, 1), 0, top)
    return jnp.take_along_axis(table, (jnp.arange(top)[None, :] + rotation) % top, axis=1)


def load_shares(count, total, most, skew, full):
    portions = [(1 << 20) // math.isqrt(grade ** skew) + 1 for grade in range(1, count + 1)]
    largest = most if full else min(most, max(-(-total // count), total * portions[0] // sum(portions)))
    least = 1 if total - largest >= count - 1 else 0
    counts, spare = [largest] + [least] * (count - 1), total - largest - least * (count - 1)
    while spare > 0:
        candidates = [i for i in range(1, count) if counts[i] < largest] or [i for i in range(1, count) if counts[i] < most]
        mass, remaining = sum([portions[i] for i in candidates]), spare
        for i in candidates:
            extra = min(most - counts[i], max(1, remaining * portions[i] // mass), spare)
            counts[i] = counts[i] + extra
            spare = spare - extra
    return np.array(counts)


def normal_values(own_key, extent, spread, reach, cuts=(), held_as=jnp.bfloat16):
    array = jax.random.normal(own_key, extent, jnp.float32) * spread
    if len(cuts) > 0:
        array = block_levels(own_key, extent, cuts, -0.22, 0.18) * array
    return jnp.clip(array, min=-reach, max=reach).astype(held_as)


def setup_inputs(seed: int = 0, part: int = 0) -> dict:
    keys = jax.random.split(jax.random.key(seed), 11)
    part_keys = jax.random.split(jax.random.fold_in(keys[10], part), 11)
    moe_rows = normal_values(part_keys[0], (TOKENS, D), 1.0, 6.0, ((0, 16),))
    expert_ids_keys = jax.random.split(jax.random.fold_in(part_keys[1], 1), TOKENS // TOK_DEV)
    expert_ids_turns = jax.random.permutation(jax.random.fold_in(part_keys[1], 3), TOKENS // TOK_DEV)
    expert_ids = jax.vmap(lambda own, number: deal_out(jax.random.fold_in(part_keys[1], 2), own, number, TOK_DEV, EXPERTS, TOPK, CAP, 2))(expert_ids_keys, expert_ids_turns).reshape((TOKENS, TOPK))
    expert_weights = jnp.clip(0.05 + 0.45 * jax.random.uniform(part_keys[2], (TOKENS, TOPK), jnp.float32) ** block_levels(part_keys[2], (TOKENS, TOPK), ((0, 16),), -0.2, 0.2), 0.05, 0.5)
    w_gate = normal_values(keys[3], (EXPERTS, D, FF), D ** -0.5, 0.0625, ((0, 4), (2, 4)))
    w_up = normal_values(keys[4], (EXPERTS, D, FF), D ** -0.5, 0.0625, ((0, 4), (2, 4)))
    w_down = normal_values(keys[5], (EXPERTS, FF, D), FF ** -0.5, 0.1875, ((0, 4), (1, 4)))
    queries = draw_queries(jax.random.fold_in(jax.random.fold_in(keys[10], part), 71), part)
    latent_cache = draw_latent_cache(jax.random.fold_in(jax.random.fold_in(keys[10], part), 71), part)
    cache_lengths = draw_cache_lengths(jax.random.fold_in(jax.random.fold_in(keys[10], part), 71), part)
    move_src = draw_move_src(jax.random.fold_in(jax.random.fold_in(keys[10], part), 71), part)
    return {"moe_rows": moe_rows, "expert_ids": expert_ids, "expert_weights": expert_weights, "w_gate": w_gate, "w_up": w_up, "w_down": w_down, "queries": queries, "latent_cache": latent_cache, "cache_lengths": cache_lengths, "move_src": move_src}


score_scale = 192.0 ** -0.5


def attend(query_rows, cache_rows, lengths):
    scores = jnp.einsum("rhc,rtc->rht", query_rows.astype(jnp.float32), cache_rows.astype(jnp.float32)) * score_scale
    places = jnp.arange(cache_rows.shape[1], dtype=jnp.int32)
    visible = places[None, None, :] < lengths[:, None, None]
    scores = jnp.where(visible, scores, -jnp.inf)
    highest = jnp.max(scores, axis=2, keepdims=True)
    powers = jnp.exp(scores - highest)
    softmax_weights = (powers / jnp.sum(powers, axis=2, keepdims=True)).astype(jnp.bfloat16)
    softmax_weights = lax.optimization_barrier(softmax_weights).astype(jnp.float32)
    latent_part = cache_rows[:, :, :LAT].astype(jnp.float32)
    return jnp.einsum("rht,rtc->rhc", softmax_weights, latent_part).astype(jnp.bfloat16)


def reference(moe_rows, expert_ids, expert_weights, w_gate, w_up, w_down, queries, latent_cache, cache_lengths, move_src):
    model_width = moe_rows.shape[1]
    flat_ids = expert_ids.reshape(-1)
    routes = TOKENS * TOPK
    row_owner = jnp.arange(routes, dtype=jnp.int32) // TOPK
    slot_bound = N_EXPERT * N_REPLICA * CAP

    def one_expert(running, expert):
        chosen = flat_ids == expert
        slot_rank = jnp.cumsum(chosen.astype(jnp.int32)) - 1
        target = jnp.where(chosen, slot_rank, slot_bound).astype(jnp.int32)
        row_index = jnp.zeros((slot_bound,), jnp.int32).at[target].set(jnp.arange(routes, dtype=jnp.int32), mode="drop")
        routed = moe_rows[row_owner[row_index]]
        gate_out = jnp.dot(routed, w_gate[expert], preferred_element_type=jnp.float32)
        up_out = jnp.dot(routed, w_up[expert], preferred_element_type=jnp.float32)
        hidden = (jax.nn.silu(gate_out) * up_out).astype(jnp.bfloat16)
        expert_out = jnp.dot(hidden, w_down[expert], preferred_element_type=jnp.float32).astype(jnp.bfloat16)
        expert_out = lax.optimization_barrier(expert_out).astype(jnp.float32)
        filled = jnp.arange(slot_bound, dtype=jnp.int32) < jnp.sum(chosen.astype(jnp.int32))
        expert_out = jnp.where(filled[:, None], expert_out, jnp.zeros_like(expert_out))
        return running.at[row_index].add(expert_out), None

    running, unused = lax.scan(one_expert, jnp.zeros((routes, model_width), jnp.float32), jnp.arange(EXPERTS, dtype=jnp.int32))
    moe_out = jnp.sum(running.reshape(TOKENS, TOPK, model_width) * expert_weights[:, :, None], axis=1).astype(jnp.bfloat16)

    source = (jnp.arange(REQS, dtype=jnp.int32) // GROUP_REQ) * GROUP_REQ + move_src
    context = attend(queries, latent_cache[source], cache_lengths[source])
    return moe_out, context
```

```python
import jax
import jax.numpy as jnp
from jax import lax
from jax.sharding import PartitionSpec as P

LAT = 512


score_scale = 192.0 ** (-0.5)


def attend(query_rows, cache_rows, lengths):
    scores = (
        jnp.einsum("rhc,rtc->rht", query_rows, cache_rows, preferred_element_type=jnp.float32)
        * score_scale
    )
    places = jnp.arange(cache_rows.shape[1], dtype=jnp.int32)
    visible = places[None, None, :] < lengths[:, None, None]
    scores = jnp.where(visible, scores, -jnp.inf)
    highest = jnp.max(scores, axis=2, keepdims=True)
    powers = jnp.exp(scores - highest)
    softmax_weights = (powers / jnp.sum(powers, axis=2, keepdims=True)).astype(jnp.bfloat16)
    return jnp.einsum(
        "rht,rtc->rhc", softmax_weights, cache_rows[:, :, :LAT], preferred_element_type=jnp.float32
    ).astype(jnp.bfloat16)


def pick(stack, places):
    return jnp.concatenate(
        [lax.dynamic_slice_in_dim(stack, places[i], 1, axis=0) for i in range(places.shape[0])],
        axis=0,
    )


def local(
    moe_rows,
    expert_ids,
    expert_weights,
    w_gate,
    w_up,
    w_down,
    queries,
    latent_cache,
    cache_lengths,
    move_src,
):
    n_expert = lax.axis_size("expert")
    n_dev = n_expert * lax.axis_size("replica")
    tokens = expert_ids.shape[0]
    model_width = moe_rows.shape[1]
    local_experts = w_gate.shape[0]
    experts = local_experts * n_expert
    both = ("expert", "replica")
    onehot = expert_ids[:, :, None] == jnp.arange(experts, dtype=jnp.int32)
    combine = jnp.sum(jnp.where(onehot, expert_weights[:, :, None], 0.0), axis=1)
    rows = lax.all_gather(moe_rows, both, axis=0, tiled=True)
    combine = lax.all_gather(combine, both, axis=0, tiled=True)
    mine = lax.dynamic_slice_in_dim(
        combine, lax.axis_index("expert") * local_experts, local_experts, axis=1
    )
    gate = jnp.einsum("nd,edf->enf", rows, w_gate, preferred_element_type=jnp.float32)
    up = jnp.einsum("nd,edf->enf", rows, w_up, preferred_element_type=jnp.float32)
    hidden = (jax.nn.silu(gate) * up * mine.T[:, :, None]).astype(jnp.bfloat16)
    partial = jnp.einsum("enf,efd->nd", hidden, w_down, preferred_element_type=jnp.float32)
    partial = partial.astype(jnp.bfloat16).reshape(n_dev, tokens, model_width)
    arrived = lax.all_to_all(partial, both, split_axis=0, concat_axis=0, tiled=True)
    moe_out = jnp.sum(arrived.astype(jnp.float32), axis=0).astype(jnp.bfloat16)

    requests = latent_cache.shape[0]
    all_queries = lax.all_gather(queries, "replica", axis=0, tiled=True)
    all_src = lax.all_gather(move_src, "replica", axis=0, tiled=True)
    held = lax.axis_index("replica") * requests + jnp.arange(requests, dtype=jnp.int32)
    count = all_src.shape[0]
    users = jnp.sum(
        jnp.where(all_src[None, :] == held[:, None], jnp.arange(count, dtype=jnp.int32), 0), axis=1
    )
    here = attend(pick(all_queries, users), latent_cache, cache_lengths)
    context = pick(lax.all_gather(here, "replica", axis=0, tiled=True), move_src)
    return (moe_out, context)


def solution(mesh):
    return jax.shard_map(
        local,
        mesh=mesh,
        in_specs=(
            P(("groups", "expert", "replica"), None),
            P(("groups", "expert", "replica"), None),
            P(("groups", "expert", "replica"), None),
            P("expert", None, "replica"),
            P("expert", None, "replica"),
            P("expert", "replica", None),
            P(("groups", "expert", "replica"), None, None),
            P(("groups", "expert", "replica"), None, None),
            P(("groups", "expert", "replica")),
            P(("groups", "expert", "replica")),
        ),
        out_specs=(
            P(("groups", "expert", "replica"), None),
            P(("groups", "expert", "replica"), None, None),
        ),
        check_vma=False,
    )
```

```python
import functools

import jax
import jax.numpy as jnp
from jax import lax
from jax.experimental import pallas as pl
from jax.experimental.pallas import tpu as pltpu
from jax.sharding import PartitionSpec as P

LAT = 512


score_scale = 192.0 ** (-0.5)


def attend(query_rows, cache_rows, lengths):
    scores = (
        jnp.einsum("rhc,rtc->rht", query_rows, cache_rows, preferred_element_type=jnp.float32)
        * score_scale
    )
    places = jnp.arange(cache_rows.shape[1], dtype=jnp.int32)
    visible = places[None, None, :] < lengths[:, None, None]
    scores = jnp.where(visible, scores, -jnp.inf)
    highest = jnp.max(scores, axis=2, keepdims=True)
    powers = jnp.exp(scores - highest)
    softmax_weights = (powers / jnp.sum(powers, axis=2, keepdims=True)).astype(jnp.bfloat16)
    return jnp.einsum(
        "rht,rtc->rhc", softmax_weights, cache_rows[:, :, :LAT], preferred_element_type=jnp.float32
    ).astype(jnp.bfloat16)


def pick(stack, places):
    return jnp.concatenate(
        [lax.dynamic_slice_in_dim(stack, places[i], 1, axis=0) for i in range(places.shape[0])],
        axis=0,
    )


def by_collectives(
    moe_rows,
    expert_ids,
    expert_weights,
    w_gate,
    w_up,
    w_down,
    queries,
    latent_cache,
    cache_lengths,
    move_src,
):
    n_expert = lax.axis_size("expert")
    n_dev = n_expert * lax.axis_size("replica")
    tokens = expert_ids.shape[0]
    model_width = moe_rows.shape[1]
    local_experts = w_gate.shape[0]
    experts = local_experts * n_expert
    both = ("expert", "replica")
    onehot = expert_ids[:, :, None] == jnp.arange(experts, dtype=jnp.int32)
    combine = jnp.sum(jnp.where(onehot, expert_weights[:, :, None], 0.0), axis=1)
    rows = lax.all_gather(moe_rows, both, axis=0, tiled=True)
    combine = lax.all_gather(combine, both, axis=0, tiled=True)
    mine = lax.dynamic_slice_in_dim(
        combine, lax.axis_index("expert") * local_experts, local_experts, axis=1
    )
    gate = jnp.einsum("nd,edf->enf", rows, w_gate, preferred_element_type=jnp.float32)
    up = jnp.einsum("nd,edf->enf", rows, w_up, preferred_element_type=jnp.float32)
    hidden = (jax.nn.silu(gate) * up * mine.T[:, :, None]).astype(jnp.bfloat16)
    partial = jnp.einsum("enf,efd->nd", hidden, w_down, preferred_element_type=jnp.float32)
    partial = partial.astype(jnp.bfloat16).reshape(n_dev, tokens, model_width)
    arrived = lax.all_to_all(partial, both, split_axis=0, concat_axis=0, tiled=True)
    moe_out = jnp.sum(arrived.astype(jnp.float32), axis=0).astype(jnp.bfloat16)

    requests = latent_cache.shape[0]
    all_queries = lax.all_gather(queries, "replica", axis=0, tiled=True)
    all_src = lax.all_gather(move_src, "replica", axis=0, tiled=True)
    held = lax.axis_index("replica") * requests + jnp.arange(requests, dtype=jnp.int32)
    count = all_src.shape[0]
    users = jnp.sum(
        jnp.where(all_src[None, :] == held[:, None], jnp.arange(count, dtype=jnp.int32), 0), axis=1
    )
    here = attend(pick(all_queries, users), latent_cache, cache_lengths)
    context = pick(lax.all_gather(here, "replica", axis=0, tiled=True), move_src)
    return (moe_out, context)


MESH = pl.DeviceIdType.MESH
CHUNKS = 8
DEPTH = 4
DOWN_DEPTH = 3


def fused_kernel(
    n_expert,
    lengths_ref,
    own_src_ref,
    src_ref,
    rows_ref,
    queries_ref,
    cache_ref,
    wg_ref,
    wu_ref,
    wd_ref,
    out_ref,
    context_ref,
    rows_all,
    x32,
    xb,
    gate_buf,
    up_buf,
    down_buf,
    hid,
    y,
    sum_a,
    send_b,
    sum_b,
    y16,
    send_c,
    sum_c,
    q_all,
    src_all,
    src_smem,
    ctx_all,
    gate_sem,
    up_sem,
    down_sem,
    row_send_z,
    row_send_2,
    row_send_1,
    row_recv,
    q_send,
    q_recv,
    src_send,
    src_recv,
    src_local,
    ctx_send,
    ctx_recv,
    a_send,
    a_recv,
    b_send,
    b_recv,
    c_send,
    c_recv,
):
    me_e = lax.axis_index("expert")
    me_r = lax.axis_index("replica")
    r2 = (me_r + 2) % 4
    r1 = me_r + 1 - 2 * (me_r % 2)
    r3 = (r1 + 2) % 4
    tokens = rows_ref.shape[0]
    local_experts, width, ff = wg_ref.shape
    experts = local_experts * n_expert
    chunk = width // CHUNKS
    band = n_expert * tokens
    requests = queries_ref.shape[0]

    def gate_copy(e):
        return pltpu.make_async_copy(
            wg_ref.at[e], gate_buf.at[e % DEPTH], gate_sem.at[e % DEPTH]
        )

    def up_copy(e):
        return pltpu.make_async_copy(wu_ref.at[e], up_buf.at[e % DEPTH], up_sem.at[e % DEPTH])

    def down_copy(c):
        return pltpu.make_async_copy(
            wd_ref.at[:, :, pl.ds(pl.multiple_of(c * chunk, 128), chunk)],
            down_buf.at[c % DOWN_DEPTH],
            down_sem.at[c % DOWN_DEPTH],
        )

    for e in range(DEPTH):
        gate_copy(e).start()
        up_copy(e).start()
    for c in range(DOWN_DEPTH):
        down_copy(c).start()

    barrier = pltpu.get_barrier_semaphore()
    for d in range(1, n_expert):
        pl.semaphore_signal(
            barrier, inc=1, device_id={"expert": (me_e + d) % n_expert}, device_id_type=MESH
        )
    for r in (r2, r1):
        pl.semaphore_signal(barrier, inc=1, device_id={"replica": r}, device_id_type=MESH)
    pl.semaphore_wait(barrier, n_expert + 1)

    def remote(src, dst, send, recv, **where):
        return pltpu.make_async_remote_copy(
            src_ref=src,
            dst_ref=dst,
            send_sem=send,
            recv_sem=recv,
            device_id=where,
            device_id_type=MESH,
        )

    def slot(e, r):
        return rows_all.at[e * 4 + r]

    def row_z(d):
        mine = me_e * 4 + me_r
        return remote(
            rows_ref,
            rows_all.at[mine],
            row_send_z.at[d - 1],
            row_recv.at[mine],
            expert=(me_e + d) % n_expert,
        )

    def row_to(d, r, source, sems, src=None):
        at = ((me_e + d) % n_expert) * 4 + source
        return remote(
            rows_all.at[at] if src is None else src,
            rows_all.at[at],
            sems,
            row_recv.at[at],
            replica=r,
        )

    def arrived(at):
        return remote(
            rows_all.at[at], rows_all.at[at], row_send_z.at[0], row_recv.at[at], replica=r1
        )

    def block(ref, r):
        return ref.at[pl.ds(pl.multiple_of(r * requests, requests), requests)]

    sends = []

    def go(copy):
        copy.start()
        sends.append(copy)

    for d in range(1, n_expert):
        go(row_z(d))
    go(row_to(0, r2, me_r, row_send_2.at[0], rows_ref))
    go(row_to(0, r1, me_r, row_send_1.at[0], rows_ref))
    for i, r in enumerate((r2, r1)):
        go(remote(src_ref, src_all.at[me_r], src_send.at[i], src_recv.at[me_r], replica=r))
    rows_all[me_e * 4 + me_r] = rows_ref[...]
    src_all[me_r] = src_ref[...]
    q_all[pl.ds(me_r * requests, requests)] = queries_ref[...]
    for d in range(1, n_expert):
        arrived(((me_e + d) % n_expert) * 4 + me_r).wait_recv()
        go(row_to(d, r2, me_r, row_send_2.at[d]))
        go(row_to(d, r1, me_r, row_send_1.at[d]))
    for i, r in enumerate((r2, r1)):
        go(remote(queries_ref, block(q_all, me_r), q_send.at[i], q_recv.at[me_r], replica=r))
    for d in range(n_expert):
        arrived(((me_e + d) % n_expert) * 4 + r2).wait_recv()
        go(row_to(d, r1, r2, row_send_1.at[n_expert + d]))
    pltpu.make_async_copy(src_all.at[r2], src_all.at[r2], src_recv.at[r2]).wait()
    go(remote(src_all.at[r2], src_all.at[r2], src_send.at[2], src_recv.at[r2], replica=r1))
    for r in (r1, r3):
        for d in range(n_expert):
            arrived(((me_e + d) % n_expert) * 4 + r).wait_recv()

    for k, r in enumerate((me_r, r2, r1, r3)):
        for e in range(n_expert):
            x32[e * tokens : (e + 1) * tokens, :] = rows_all[e * 4 + r].astype(jnp.float32)
        xb[k * band : (k + 1) * band, :] = x32[...].astype(jnp.bfloat16)

    places = lax.broadcasted_iota(jnp.int32, (128, ff), 0)

    def first(e, carry):
        gate_copy(e).wait()
        up_copy(e).wait()
        x = xb[:, :width]
        gate = jnp.dot(x, gate_buf[e % DEPTH], preferred_element_type=jnp.float32)
        up = jnp.dot(x, up_buf[e % DEPTH], preferred_element_type=jnp.float32)
        mine = me_e * local_experts + e
        hit = (places == mine) | (places == mine + experts) | (places == mine + 2 * experts)
        weight = jnp.dot(
            xb[:, width:],
            jnp.where(hit, 1.0, 0.0).astype(jnp.bfloat16),
            preferred_element_type=jnp.float32,
        )
        hidden = (gate / (1.0 + jnp.exp(-gate)) * up).astype(jnp.bfloat16)
        hid[e] = (hidden.astype(jnp.float32) * weight).astype(jnp.bfloat16)

        @pl.when(e + DEPTH < local_experts)
        def _():
            gate_copy(e + DEPTH).start()
            up_copy(e + DEPTH).start()

        return carry

    def q_forward():
        return remote(
            block(q_all, r2), block(q_all, r2), q_send.at[2], q_recv.at[r2], replica=r1
        )

    half = local_experts // 2
    lax.fori_loop(0, half, first, 0)
    q_forward().wait_recv()
    go(q_forward())
    for r in (r1, r3):
        pltpu.make_async_copy(src_all.at[r], src_all.at[r], src_recv.at[r]).wait()
    local_src = pltpu.make_async_copy(src_all, src_smem, src_local)
    local_src.start()
    lax.fori_loop(half, local_experts, first, 0)
    local_src.wait()
    for r in (r1, r3):
        remote(block(q_all, r), block(q_all, r), q_send.at[0], q_recv.at[r], replica=r1).wait_recv()

    positions = cache_ref.shape[1]
    seen = lax.broadcasted_iota(jnp.int32, (queries_ref.shape[1], positions), 1)
    for j in range(requests):
        held = me_r * requests + j
        user = jnp.int32(0)
        for r in range(4):
            for i in range(requests):
                user = jnp.where(src_smem[r, 0, i] == held, r * requests + i, user)
        scores = (
            lax.dot_general(
                q_all[user],
                cache_ref[j],
                (((1,), (1,)), ((), ())),
                preferred_element_type=jnp.float32,
            )
            * score_scale
        )
        scores = jnp.where(seen < lengths_ref[j], scores, -jnp.inf)
        powers = jnp.exp(scores - jnp.max(scores, axis=1, keepdims=True))
        probs = (powers / jnp.sum(powers, axis=1, keepdims=True)).astype(jnp.bfloat16)
        ctx_all[me_r * requests + j] = jnp.dot(
            probs, cache_ref[j, :, :LAT], preferred_element_type=jnp.float32
        ).astype(jnp.bfloat16)
    for i, r in enumerate((r2, r1)):
        go(
            remote(
                block(ctx_all, me_r),
                block(ctx_all, me_r),
                ctx_send.at[i],
                ctx_recv.at[me_r],
                replica=r,
            )
        )

    def a_copy(c):
        return remote(
            y.at[c, pl.ds(2 * band, 2 * band)], sum_a.at[c], a_send.at[c], a_recv.at[c], replica=r1
        )

    def b_copy(c):
        return remote(send_b.at[c], sum_b.at[c], b_send.at[c], b_recv.at[c], replica=r2)

    def c_copy(c, d):
        to = (me_e + d) % n_expert
        return remote(
            send_c.at[c, to],
            sum_c.at[c, me_e],
            c_send.at[c, d - 1],
            c_recv.at[c, me_e],
            expert=to,
        )

    def c_arrived(c, d):
        at = (me_e + d) % n_expert
        return remote(
            send_c.at[c, at], sum_c.at[c, at], c_send.at[c, d - 1], c_recv.at[c, at], expert=at
        )

    def second(step, carry):
        @pl.when(step < CHUNKS)
        def _():
            down_copy(step).wait()
            total = jnp.dot(
                hid[0], down_buf[step % DOWN_DEPTH, 0], preferred_element_type=jnp.float32
            )
            for e in range(1, local_experts):
                total += jnp.dot(
                    hid[e], down_buf[step % DOWN_DEPTH, e], preferred_element_type=jnp.float32
                )
            y[step] = total
            a_copy(step).start()

            @pl.when(step + DOWN_DEPTH < CHUNKS)
            def _():
                down_copy(step + DOWN_DEPTH).start()

        @pl.when((step >= 1) & (step <= CHUNKS))
        def _():
            c = step - 1
            a_copy(c).wait_recv()
            send_b[c] = (y[c, band : 2 * band] + sum_a[c, band:]).astype(jnp.bfloat16)
            b_copy(c).start()

        @pl.when(step >= 2)
        def _():
            c = step - 2
            b_copy(c).wait_recv()
            y16[...] = y[c, :band] + sum_a[c, :band] + sum_b[c].astype(jnp.float32)
            for e in range(n_expert):
                send_c[c, e] = y16[e * tokens : (e + 1) * tokens].astype(jnp.bfloat16)
            for d in range(1, n_expert):
                c_copy(c, d).start()

        return carry

    def ctx_forward():
        return remote(
            block(ctx_all, r2), block(ctx_all, r2), ctx_send.at[2], ctx_recv.at[r2], replica=r1
        )

    lax.fori_loop(0, CHUNKS - 1, second, 0)
    ctx_forward().wait_recv()
    go(ctx_forward())
    lax.fori_loop(CHUNKS - 1, CHUNKS + 2, second, 0)

    for r in (r1, r3):
        remote(
            block(ctx_all, r), block(ctx_all, r), ctx_send.at[0], ctx_recv.at[r], replica=r1
        ).wait_recv()
    for j in range(requests):
        context_ref[j] = ctx_all[own_src_ref[j]]
    for c in range(CHUNKS):
        total = send_c[c, me_e].astype(jnp.float32)
        for d in range(1, n_expert):
            c_arrived(c, d).wait_recv()
            total += sum_c[c, (me_e + d) % n_expert].astype(jnp.float32)
        out_ref[:, c * chunk : (c + 1) * chunk] = total.astype(jnp.bfloat16)

    for copy in sends:
        copy.wait_send()

    def drain(c, carry):
        a_copy(c).wait_send()
        b_copy(c).wait_send()
        for d in range(1, n_expert):
            c_copy(c, d).wait_send()
        return carry

    lax.fori_loop(0, CHUNKS, drain, 0)


def fused(
    moe_rows,
    expert_ids,
    expert_weights,
    w_gate,
    w_up,
    w_down,
    queries,
    latent_cache,
    cache_lengths,
    move_src,
):
    n_expert = lax.axis_size("expert")
    tokens = expert_ids.shape[0]
    local_experts, width, ff = w_gate.shape
    experts = local_experts * n_expert
    requests, heads, channels = queries.shape
    onehot = expert_ids[:, :, None] == jnp.arange(experts, dtype=jnp.int32)
    combine = jnp.sum(jnp.where(onehot, expert_weights[:, :, None], 0.0), axis=1)
    pieces = []
    rest = combine
    for _ in range(3):
        piece = lax.reduce_precision(rest, 8, 7)
        pieces.append(piece.astype(jnp.bfloat16))
        rest = rest - piece
    spare = 128 - 3 * experts
    rows = jnp.concatenate(
        [moe_rows] + pieces + [jnp.zeros((tokens, spare), jnp.bfloat16)], axis=1
    )
    src_block = jnp.zeros((8, 128), jnp.int32).at[0, :requests].set(move_src)
    chunk = width // CHUNKS
    band = n_expert * tokens
    n = 4 * band
    bf16, f32 = jnp.bfloat16, jnp.float32
    vmem = pl.BlockSpec(memory_space=pltpu.VMEM)
    smem = pl.BlockSpec(memory_space=pltpu.SMEM)
    hbm = pl.BlockSpec(memory_space=pl.ANY)
    dma = pltpu.SemaphoreType.DMA
    return pl.pallas_call(
        functools.partial(fused_kernel, n_expert),
        out_shape=(
            jax.ShapeDtypeStruct((tokens, width), bf16),
            jax.ShapeDtypeStruct((requests, heads, LAT), bf16),
        ),
        in_specs=[smem, smem, vmem, vmem, vmem, vmem, hbm, hbm, hbm],
        out_specs=(vmem, vmem),
        scratch_shapes=[
            pltpu.VMEM((4 * n_expert, tokens, width + 128), bf16),
            pltpu.VMEM((band, width + 128), f32),
            pltpu.VMEM((n, width + 128), bf16),
            pltpu.VMEM((DEPTH, width, ff), bf16),
            pltpu.VMEM((DEPTH, width, ff), bf16),
            pltpu.VMEM((DOWN_DEPTH, local_experts, ff, chunk), bf16),
            pltpu.VMEM((local_experts, n, ff), bf16),
            pltpu.VMEM((CHUNKS, n, chunk), f32),
            pltpu.VMEM((CHUNKS, 2 * band, chunk), f32),
            pltpu.VMEM((CHUNKS, band, chunk), bf16),
            pltpu.VMEM((CHUNKS, band, chunk), bf16),
            pltpu.VMEM((band, chunk), f32),
            pltpu.VMEM((CHUNKS, n_expert, tokens, chunk), bf16),
            pltpu.VMEM((CHUNKS, n_expert, tokens, chunk), bf16),
            pltpu.VMEM((4 * requests, heads, channels), bf16),
            pltpu.VMEM((4, 8, 128), jnp.int32),
            pltpu.SMEM((4, 8, 128), jnp.int32),
            pltpu.VMEM((4 * requests, heads, LAT), bf16),
            dma((DEPTH,)),
            dma((DEPTH,)),
            dma((DOWN_DEPTH,)),
            dma((n_expert,)),
            dma((n_expert,)),
            dma((2 * n_expert,)),
            dma((4 * n_expert,)),
            dma((3,)),
            dma((4,)),
            dma((3,)),
            dma((4,)),
            dma,
            dma((3,)),
            dma((4,)),
            dma((CHUNKS,)),
            dma((CHUNKS,)),
            dma((CHUNKS,)),
            dma((CHUNKS,)),
            dma((CHUNKS, n_expert)),
            dma((CHUNKS, n_expert)),
        ],
        compiler_params=pltpu.CompilerParams(
            collective_id=0, has_side_effects=True, vmem_limit_bytes=62 * 1024 * 1024
        ),
    )(
        cache_lengths,
        move_src,
        src_block,
        rows,
        queries,
        latent_cache,
        w_gate,
        w_up,
        w_down,
    )


def local(*arrays):
    n_expert, n_replica = lax.axis_size("expert"), lax.axis_size("replica")
    tokens = arrays[0].shape[0]
    local_experts = arrays[3].shape[0]
    small = (
        n_replica == 4
        and n_expert * tokens == 16
        and local_experts >= DEPTH
        and local_experts % 2 == 0
        and 3 * local_experts * n_expert <= 128
    )
    return fused(*arrays) if small else by_collectives(*arrays)


def solution(mesh):
    return jax.shard_map(
        local,
        mesh=mesh,
        in_specs=(
            P(("groups", "expert", "replica"), None),
            P(("groups", "expert", "replica"), None),
            P(("groups", "expert", "replica"), None),
            P("expert", None, "replica"),
            P("expert", None, "replica"),
            P("expert", "replica", None),
            P(("groups", "expert", "replica"), None, None),
            P(("groups", "expert", "replica"), None, None),
            P(("groups", "expert", "replica")),
            P(("groups", "expert", "replica")),
        ),
        out_specs=(
            P(("groups", "expert", "replica"), None),
            P(("groups", "expert", "replica"), None, None),
        ),
        check_vma=False,
    )
```

```python
import functools

import jax
import jax.numpy as jnp
from jax import lax
from jax.experimental import pallas as pl
from jax.experimental.pallas import tpu as pltpu
from jax.sharding import PartitionSpec as P

LAT = 512


score_scale = 192.0 ** (-0.5)


def attend(query_rows, cache_rows, lengths):
    scores = (
        jnp.einsum("rhc,rtc->rht", query_rows, cache_rows, preferred_element_type=jnp.float32)
        * score_scale
    )
    places = jnp.arange(cache_rows.shape[1], dtype=jnp.int32)
    visible = places[None, None, :] < lengths[:, None, None]
    scores = jnp.where(visible, scores, -jnp.inf)
    highest = jnp.max(scores, axis=2, keepdims=True)
    powers = jnp.exp(scores - highest)
    softmax_weights = (powers / jnp.sum(powers, axis=2, keepdims=True)).astype(jnp.bfloat16)
    return jnp.einsum(
        "rht,rtc->rhc", softmax_weights, cache_rows[:, :, :LAT], preferred_element_type=jnp.float32
    ).astype(jnp.bfloat16)


def pick(stack, places):
    return jnp.concatenate(
        [lax.dynamic_slice_in_dim(stack, places[i], 1, axis=0) for i in range(places.shape[0])],
        axis=0,
    )


def by_collectives(
    moe_rows,
    expert_ids,
    expert_weights,
    w_gate,
    w_up,
    w_down,
    queries,
    latent_cache,
    cache_lengths,
    move_src,
):
    n_expert = lax.axis_size("expert")
    n_dev = n_expert * lax.axis_size("replica")
    tokens = expert_ids.shape[0]
    model_width = moe_rows.shape[1]
    local_experts = w_gate.shape[0]
    experts = local_experts * n_expert
    both = ("expert", "replica")
    onehot = expert_ids[:, :, None] == jnp.arange(experts, dtype=jnp.int32)
    combine = jnp.sum(jnp.where(onehot, expert_weights[:, :, None], 0.0), axis=1)
    rows = lax.all_gather(moe_rows, both, axis=0, tiled=True)
    combine = lax.all_gather(combine, both, axis=0, tiled=True)
    mine = lax.dynamic_slice_in_dim(
        combine, lax.axis_index("expert") * local_experts, local_experts, axis=1
    )
    gate = jnp.einsum("nd,edf->enf", rows, w_gate, preferred_element_type=jnp.float32)
    up = jnp.einsum("nd,edf->enf", rows, w_up, preferred_element_type=jnp.float32)
    hidden = (jax.nn.silu(gate) * up * mine.T[:, :, None]).astype(jnp.bfloat16)
    partial = jnp.einsum("enf,efd->nd", hidden, w_down, preferred_element_type=jnp.float32)
    partial = partial.astype(jnp.bfloat16).reshape(n_dev, tokens, model_width)
    arrived = lax.all_to_all(partial, both, split_axis=0, concat_axis=0, tiled=True)
    moe_out = jnp.sum(arrived.astype(jnp.float32), axis=0).astype(jnp.bfloat16)

    requests = latent_cache.shape[0]
    all_queries = lax.all_gather(queries, "replica", axis=0, tiled=True)
    all_src = lax.all_gather(move_src, "replica", axis=0, tiled=True)
    held = lax.axis_index("replica") * requests + jnp.arange(requests, dtype=jnp.int32)
    count = all_src.shape[0]
    users = jnp.sum(
        jnp.where(all_src[None, :] == held[:, None], jnp.arange(count, dtype=jnp.int32), 0), axis=1
    )
    here = attend(pick(all_queries, users), latent_cache, cache_lengths)
    context = pick(lax.all_gather(here, "replica", axis=0, tiled=True), move_src)
    return (moe_out, context)


MESH = pl.DeviceIdType.MESH
CHUNKS = 8
DEPTH = 4
DOWN_DEPTH = 3
LAG = 2


def fused_kernel(
    n_expert,
    lengths_ref,
    own_src_ref,
    ids_ref,
    weights_ref,
    rows_ref,
    queries_ref,
    cache_hbm,
    wg_ref,
    wu_ref,
    wd_ref,
    out_ref,
    context_ref,
    rows_all,
    x32,
    xb,
    gate_buf,
    up_buf,
    down_buf,
    hid,
    y,
    sum_a,
    send_b,
    sum_b,
    y16,
    send_c,
    sum_c,
    q_all,
    src_all,
    src_smem,
    ctx_all,
    cache_ref,
    q_local,
    cache_local,
    gate_sem,
    up_sem,
    down_sem,
    row_send_z,
    row_send_2,
    row_send_1,
    row_recv,
    q_send,
    q_recv,
    src_send,
    src_recv,
    src_local,
    ctx_send,
    ctx_recv,
    a_send,
    a_recv,
    b_send,
    b_recv,
    c_send,
    c_recv,
):
    me_e = lax.axis_index("expert")
    me_r = lax.axis_index("replica")
    r2 = (me_r + 2) % 4
    r1 = me_r + 1 - 2 * (me_r % 2)
    r3 = (r1 + 2) % 4
    tokens = rows_ref.shape[0]
    local_experts, width, ff = wg_ref.shape
    experts = local_experts * n_expert
    chunk = width // CHUNKS
    band = n_expert * tokens
    requests = queries_ref.shape[0]

    def gate_copy(e):
        return pltpu.make_async_copy(
            wg_ref.at[e], gate_buf.at[e % DEPTH], gate_sem.at[e % DEPTH]
        )

    def up_copy(e):
        return pltpu.make_async_copy(wu_ref.at[e], up_buf.at[e % DEPTH], up_sem.at[e % DEPTH])

    def down_copy(c):
        return pltpu.make_async_copy(
            wd_ref.at[:, :, pl.ds(pl.multiple_of(c * chunk, 128), chunk)],
            down_buf.at[c % DOWN_DEPTH],
            down_sem.at[c % DOWN_DEPTH],
        )

    own_q = pltpu.make_async_copy(
        queries_ref,
        q_all.at[pl.ds(pl.multiple_of(me_r * requests, requests), requests)],
        q_local,
    )
    own_cache = pltpu.make_async_copy(cache_hbm, cache_ref, cache_local)
    own_q.start()
    own_cache.start()
    for e in range(DEPTH):
        gate_copy(e).start()
        up_copy(e).start()
    for c in range(DOWN_DEPTH):
        down_copy(c).start()

    mine = me_e * 4 + me_r
    lane = lax.broadcasted_iota(jnp.int32, (tokens, 128), 1)
    expert = lane % experts
    combine = jnp.zeros((tokens, 128), jnp.float32)
    for k in range(ids_ref.shape[1]):
        combine += jnp.where(ids_ref[:, k : k + 1] == expert, weights_ref[:, k : k + 1], 0.0)
    high = combine.astype(jnp.bfloat16).astype(jnp.float32)
    middle = (combine - high).astype(jnp.bfloat16).astype(jnp.float32)
    low = combine - high - middle
    pieces = jnp.where(
        lane < experts,
        high,
        jnp.where(lane < 2 * experts, middle, jnp.where(lane < 3 * experts, low, 0.0)),
    )
    rows_all[mine, :, :width] = rows_ref[...]
    rows_all[mine, :, width:] = pieces.astype(jnp.bfloat16)
    place = lax.broadcasted_iota(jnp.int32, (8, 128), 1)
    sources = jnp.zeros((8, 128), jnp.int32)
    for i in range(requests):
        sources = jnp.where(place == i, own_src_ref[i], sources)
    src_all[me_r] = sources

    barrier = pltpu.get_barrier_semaphore()
    for d in range(1, n_expert):
        pl.semaphore_signal(
            barrier, inc=1, device_id={"expert": (me_e + d) % n_expert}, device_id_type=MESH
        )
    for r in (r2, r1):
        pl.semaphore_signal(barrier, inc=1, device_id={"replica": r}, device_id_type=MESH)
    pl.semaphore_wait(barrier, n_expert + 1)

    def remote(src, dst, send, recv, **where):
        return pltpu.make_async_remote_copy(
            src_ref=src,
            dst_ref=dst,
            send_sem=send,
            recv_sem=recv,
            device_id=where,
            device_id_type=MESH,
        )

    def slot(e, r):
        return rows_all.at[e * 4 + r]

    def row_z(d):
        return remote(
            rows_all.at[mine],
            rows_all.at[mine],
            row_send_z.at[d - 1],
            row_recv.at[mine],
            expert=(me_e + d) % n_expert,
        )

    def row_to(d, r, source, sems):
        at = ((me_e + d) % n_expert) * 4 + source
        return remote(
            rows_all.at[at],
            rows_all.at[at],
            sems,
            row_recv.at[at],
            replica=r,
        )

    def arrived(at):
        return remote(
            rows_all.at[at], rows_all.at[at], row_send_z.at[0], row_recv.at[at], replica=r1
        )

    def block(ref, r):
        return ref.at[pl.ds(pl.multiple_of(r * requests, requests), requests)]

    sends = []

    def go(copy):
        copy.start()
        sends.append(copy)

    for d in range(1, n_expert):
        go(row_z(d))
    go(row_to(0, r2, me_r, row_send_2.at[0]))
    go(row_to(0, r1, me_r, row_send_1.at[0]))
    for i, r in enumerate((r2, r1)):
        go(remote(src_all.at[me_r], src_all.at[me_r], src_send.at[i], src_recv.at[me_r], replica=r))
    for d in range(1, n_expert):
        arrived(((me_e + d) % n_expert) * 4 + me_r).wait_recv()
        go(row_to(d, r2, me_r, row_send_2.at[d]))
        go(row_to(d, r1, me_r, row_send_1.at[d]))
    own_q.wait()
    for i, r in enumerate((r2, r1)):
        go(remote(block(q_all, me_r), block(q_all, me_r), q_send.at[i], q_recv.at[me_r], replica=r))
    for d in range(n_expert):
        arrived(((me_e + d) % n_expert) * 4 + r2).wait_recv()
        go(row_to(d, r1, r2, row_send_1.at[n_expert + d]))
    pltpu.make_async_copy(src_all.at[r2], src_all.at[r2], src_recv.at[r2]).wait()
    go(remote(src_all.at[r2], src_all.at[r2], src_send.at[2], src_recv.at[r2], replica=r1))
    for r in (r1, r3):
        for d in range(n_expert):
            arrived(((me_e + d) % n_expert) * 4 + r).wait_recv()

    for k, r in enumerate((me_r, r2, r1, r3)):
        for e in range(n_expert):
            x32[e * tokens : (e + 1) * tokens, :] = rows_all[e * 4 + r].astype(jnp.float32)
        xb[k * band : (k + 1) * band, :] = x32[...].astype(jnp.bfloat16)

    places = lax.broadcasted_iota(jnp.int32, (128, ff), 0)

    def first(e, carry):
        gate_copy(e).wait()
        up_copy(e).wait()
        x = xb[:, :width]
        gate = jnp.dot(x, gate_buf[e % DEPTH], preferred_element_type=jnp.float32)
        up = jnp.dot(x, up_buf[e % DEPTH], preferred_element_type=jnp.float32)
        at = me_e * local_experts + e
        hit = (places == at) | (places == at + experts) | (places == at + 2 * experts)
        weight = jnp.dot(
            xb[:, width:],
            jnp.where(hit, 1.0, 0.0).astype(jnp.bfloat16),
            preferred_element_type=jnp.float32,
        )
        hidden = (gate / (1.0 + jnp.exp(-gate)) * up).astype(jnp.bfloat16)
        hid[e] = (hidden.astype(jnp.float32) * weight).astype(jnp.bfloat16)

        @pl.when(e + DEPTH < local_experts)
        def _():
            gate_copy(e + DEPTH).start()
            up_copy(e + DEPTH).start()

        return carry

    def q_forward():
        return remote(
            block(q_all, r2), block(q_all, r2), q_send.at[2], q_recv.at[r2], replica=r1
        )

    half = local_experts // 2
    lax.fori_loop(0, half, first, 0)
    q_forward().wait_recv()
    go(q_forward())
    for r in (r1, r3):
        pltpu.make_async_copy(src_all.at[r], src_all.at[r], src_recv.at[r]).wait()
    local_src = pltpu.make_async_copy(src_all, src_smem, src_local)
    local_src.start()
    lax.fori_loop(half, local_experts, first, 0)
    local_src.wait()
    for r in (r1, r3):
        remote(block(q_all, r), block(q_all, r), q_send.at[0], q_recv.at[r], replica=r1).wait_recv()

    own_cache.wait()
    positions = cache_ref.shape[2]
    seen = lax.broadcasted_iota(jnp.int32, (queries_ref.shape[1], positions), 1)
    for j in range(requests):
        held = me_r * requests + j
        user = jnp.int32(0)
        for r in range(4):
            for i in range(requests):
                user = jnp.where(src_smem[r, 0, i] == held, r * requests + i, user)
        scores = (
            lax.dot_general(
                q_all[user],
                cache_ref[j],
                (((1,), (0,)), ((), ())),
                preferred_element_type=jnp.float32,
            )
            * score_scale
        )
        scores = jnp.where(seen < lengths_ref[j], scores, -jnp.inf)
        powers = jnp.exp(scores - jnp.max(scores, axis=1, keepdims=True))
        probs = (powers / jnp.sum(powers, axis=1, keepdims=True)).astype(jnp.bfloat16)
        ctx_all[me_r * requests + j] = lax.dot_general(
            probs,
            cache_ref[j, :LAT, :],
            (((1,), (1,)), ((), ())),
            preferred_element_type=jnp.float32,
        ).astype(jnp.bfloat16)
    for i, r in enumerate((r2, r1)):
        go(
            remote(
                block(ctx_all, me_r),
                block(ctx_all, me_r),
                ctx_send.at[i],
                ctx_recv.at[me_r],
                replica=r,
            )
        )

    def a_copy(c):
        return remote(
            y.at[c, pl.ds(2 * band, 2 * band)], sum_a.at[c], a_send.at[c], a_recv.at[c], replica=r1
        )

    def b_copy(c):
        return remote(send_b.at[c], sum_b.at[c], b_send.at[c], b_recv.at[c], replica=r2)

    def c_copy(c, d):
        to = (me_e + d) % n_expert
        return remote(
            send_c.at[c, to],
            sum_c.at[c, me_e],
            c_send.at[c, d - 1],
            c_recv.at[c, me_e],
            expert=to,
        )

    def c_arrived(c, d):
        at = (me_e + d) % n_expert
        return remote(
            send_c.at[c, at], sum_c.at[c, at], c_send.at[c, d - 1], c_recv.at[c, at], expert=at
        )

    def second(step, carry):
        @pl.when(step < CHUNKS)
        def _():
            down_copy(step).wait()
            total = jnp.dot(
                hid[0], down_buf[step % DOWN_DEPTH, 0], preferred_element_type=jnp.float32
            )
            for e in range(1, local_experts):
                total += jnp.dot(
                    hid[e], down_buf[step % DOWN_DEPTH, e], preferred_element_type=jnp.float32
                )
            y[step] = total
            a_copy(step).start()

            @pl.when(step + DOWN_DEPTH < CHUNKS)
            def _():
                down_copy(step + DOWN_DEPTH).start()

        @pl.when((step >= LAG) & (step < CHUNKS + LAG))
        def _():
            c = step - LAG
            a_copy(c).wait_recv()
            send_b[c] = (y[c, band : 2 * band] + sum_a[c, band:]).astype(jnp.bfloat16)
            b_copy(c).start()

        @pl.when(step >= 2 * LAG)
        def _():
            c = step - 2 * LAG
            b_copy(c).wait_recv()
            y16[...] = y[c, :band] + sum_a[c, :band] + sum_b[c].astype(jnp.float32)
            for e in range(n_expert):
                send_c[c, e] = y16[e * tokens : (e + 1) * tokens].astype(jnp.bfloat16)
            for d in range(1, n_expert):
                c_copy(c, d).start()

        return carry

    def ctx_forward():
        return remote(
            block(ctx_all, r2), block(ctx_all, r2), ctx_send.at[2], ctx_recv.at[r2], replica=r1
        )

    lax.fori_loop(0, CHUNKS - 1, second, 0)
    ctx_forward().wait_recv()
    go(ctx_forward())
    lax.fori_loop(CHUNKS - 1, CHUNKS + 2 * LAG, second, 0)

    for r in (r1, r3):
        remote(
            block(ctx_all, r), block(ctx_all, r), ctx_send.at[0], ctx_recv.at[r], replica=r1
        ).wait_recv()
    for j in range(requests):
        context_ref[j] = ctx_all[own_src_ref[j]]
    for c in range(CHUNKS):
        total = send_c[c, me_e].astype(jnp.float32)
        for d in range(1, n_expert):
            c_arrived(c, d).wait_recv()
            total += sum_c[c, (me_e + d) % n_expert].astype(jnp.float32)
        out_ref[:, c * chunk : (c + 1) * chunk] = total.astype(jnp.bfloat16)

    for copy in sends:
        copy.wait_send()

    def drain(c, carry):
        a_copy(c).wait_send()
        b_copy(c).wait_send()
        for d in range(1, n_expert):
            c_copy(c, d).wait_send()
        return carry

    lax.fori_loop(0, CHUNKS, drain, 0)


def fused(
    moe_rows,
    expert_ids,
    expert_weights,
    w_gate,
    w_up,
    w_down,
    queries,
    latent_cache,
    cache_lengths,
    move_src,
):
    n_expert = lax.axis_size("expert")
    tokens = expert_ids.shape[0]
    local_experts, width, ff = w_gate.shape
    requests, heads, channels = queries.shape
    chunk = width // CHUNKS
    band = n_expert * tokens
    n = 4 * band
    bf16, f32 = jnp.bfloat16, jnp.float32
    vmem = pl.BlockSpec(memory_space=pltpu.VMEM)
    smem = pl.BlockSpec(memory_space=pltpu.SMEM)
    hbm = pl.BlockSpec(memory_space=pl.ANY)
    dma = pltpu.SemaphoreType.DMA
    return pl.pallas_call(
        functools.partial(fused_kernel, n_expert),
        out_shape=(
            jax.ShapeDtypeStruct((tokens, width), bf16),
            jax.ShapeDtypeStruct((requests, heads, LAT), bf16),
        ),
        in_specs=[smem, smem, vmem, vmem, vmem, hbm, hbm, hbm, hbm, hbm],
        out_specs=(vmem, vmem),
        scratch_shapes=[
            pltpu.VMEM((4 * n_expert, tokens, width + 128), bf16),
            pltpu.VMEM((band, width + 128), f32),
            pltpu.VMEM((n, width + 128), bf16),
            pltpu.VMEM((DEPTH, width, ff), bf16),
            pltpu.VMEM((DEPTH, width, ff), bf16),
            pltpu.VMEM((DOWN_DEPTH, local_experts, ff, chunk), bf16),
            pltpu.VMEM((local_experts, n, ff), bf16),
            pltpu.VMEM((CHUNKS, n, chunk), f32),
            pltpu.VMEM((CHUNKS, 2 * band, chunk), f32),
            pltpu.VMEM((CHUNKS, band, chunk), bf16),
            pltpu.VMEM((CHUNKS, band, chunk), bf16),
            pltpu.VMEM((band, chunk), f32),
            pltpu.VMEM((CHUNKS, n_expert, tokens, chunk), bf16),
            pltpu.VMEM((CHUNKS, n_expert, tokens, chunk), bf16),
            pltpu.VMEM((4 * requests, heads, channels), bf16),
            pltpu.VMEM((4, 8, 128), jnp.int32),
            pltpu.SMEM((4, 8, 128), jnp.int32),
            pltpu.VMEM((4 * requests, heads, LAT), bf16),
            pltpu.VMEM((requests, channels, latent_cache.shape[1]), bf16),
            dma,
            dma,
            dma((DEPTH,)),
            dma((DEPTH,)),
            dma((DOWN_DEPTH,)),
            dma((n_expert,)),
            dma((n_expert,)),
            dma((2 * n_expert,)),
            dma((4 * n_expert,)),
            dma((3,)),
            dma((4,)),
            dma((3,)),
            dma((4,)),
            dma,
            dma((3,)),
            dma((4,)),
            dma((CHUNKS,)),
            dma((CHUNKS,)),
            dma((CHUNKS,)),
            dma((CHUNKS,)),
            dma((CHUNKS, n_expert)),
            dma((CHUNKS, n_expert)),
        ],
        compiler_params=pltpu.CompilerParams(
            collective_id=0, has_side_effects=True, vmem_limit_bytes=62 * 1024 * 1024
        ),
    )(
        cache_lengths,
        move_src,
        expert_ids,
        expert_weights,
        moe_rows,
        queries,
        jnp.swapaxes(latent_cache, 1, 2),
        w_gate,
        w_up,
        w_down,
    )


def local(*arrays):
    n_expert, n_replica = lax.axis_size("expert"), lax.axis_size("replica")
    tokens = arrays[0].shape[0]
    local_experts = arrays[3].shape[0]
    small = (
        n_replica == 4
        and n_expert * tokens == 16
        and local_experts >= DEPTH
        and local_experts % 2 == 0
        and 3 * local_experts * n_expert <= 128
    )
    return fused(*arrays) if small else by_collectives(*arrays)


def solution(mesh):
    return jax.shard_map(
        local,
        mesh=mesh,
        in_specs=(
            P(("groups", "expert", "replica"), None),
            P(("groups", "expert", "replica"), None),
            P(("groups", "expert", "replica"), None),
            P("expert", None, "replica"),
            P("expert", None, "replica"),
            P("expert", "replica", None),
            P(("groups", "expert", "replica"), None, None),
            P(("groups", "expert", "replica"), None, None),
            P(("groups", "expert", "replica")),
            P(("groups", "expert", "replica")),
        ),
        out_specs=(
            P(("groups", "expert", "replica"), None),
            P(("groups", "expert", "replica"), None, None),
        ),
        check_vma=False,
    )
```

```python
import functools

import jax
import jax.numpy as jnp
from jax import lax
from jax.experimental import pallas as pl
from jax.experimental.pallas import tpu as pltpu
from jax.sharding import PartitionSpec as P

LAT = 512


score_scale = 192.0 ** (-0.5)


def attend(query_rows, cache_rows, lengths):
    scores = (
        jnp.einsum("rhc,rtc->rht", query_rows, cache_rows, preferred_element_type=jnp.float32)
        * score_scale
    )
    places = jnp.arange(cache_rows.shape[1], dtype=jnp.int32)
    visible = places[None, None, :] < lengths[:, None, None]
    scores = jnp.where(visible, scores, -jnp.inf)
    highest = jnp.max(scores, axis=2, keepdims=True)
    powers = jnp.exp(scores - highest)
    softmax_weights = (powers / jnp.sum(powers, axis=2, keepdims=True)).astype(jnp.bfloat16)
    return jnp.einsum(
        "rht,rtc->rhc", softmax_weights, cache_rows[:, :, :LAT], preferred_element_type=jnp.float32
    ).astype(jnp.bfloat16)


def pick(stack, places):
    return jnp.concatenate(
        [lax.dynamic_slice_in_dim(stack, places[i], 1, axis=0) for i in range(places.shape[0])],
        axis=0,
    )


def by_collectives(
    moe_rows,
    expert_ids,
    expert_weights,
    w_gate,
    w_up,
    w_down,
    queries,
    latent_cache,
    cache_lengths,
    move_src,
):
    n_expert = lax.axis_size("expert")
    n_dev = n_expert * lax.axis_size("replica")
    tokens = expert_ids.shape[0]
    model_width = moe_rows.shape[1]
    local_experts = w_gate.shape[0]
    experts = local_experts * n_expert
    both = ("expert", "replica")
    onehot = expert_ids[:, :, None] == jnp.arange(experts, dtype=jnp.int32)
    combine = jnp.sum(jnp.where(onehot, expert_weights[:, :, None], 0.0), axis=1)
    rows = lax.all_gather(moe_rows, both, axis=0, tiled=True)
    combine = lax.all_gather(combine, both, axis=0, tiled=True)
    mine = lax.dynamic_slice_in_dim(
        combine, lax.axis_index("expert") * local_experts, local_experts, axis=1
    )
    gate = jnp.einsum("nd,edf->enf", rows, w_gate, preferred_element_type=jnp.float32)
    up = jnp.einsum("nd,edf->enf", rows, w_up, preferred_element_type=jnp.float32)
    hidden = (jax.nn.silu(gate) * up * mine.T[:, :, None]).astype(jnp.bfloat16)
    partial = jnp.einsum("enf,efd->nd", hidden, w_down, preferred_element_type=jnp.float32)
    partial = partial.astype(jnp.bfloat16).reshape(n_dev, tokens, model_width)
    arrived = lax.all_to_all(partial, both, split_axis=0, concat_axis=0, tiled=True)
    moe_out = jnp.sum(arrived.astype(jnp.float32), axis=0).astype(jnp.bfloat16)

    requests = latent_cache.shape[0]
    all_queries = lax.all_gather(queries, "replica", axis=0, tiled=True)
    all_src = lax.all_gather(move_src, "replica", axis=0, tiled=True)
    held = lax.axis_index("replica") * requests + jnp.arange(requests, dtype=jnp.int32)
    count = all_src.shape[0]
    users = jnp.sum(
        jnp.where(all_src[None, :] == held[:, None], jnp.arange(count, dtype=jnp.int32), 0), axis=1
    )
    here = attend(pick(all_queries, users), latent_cache, cache_lengths)
    context = pick(lax.all_gather(here, "replica", axis=0, tiled=True), move_src)
    return (moe_out, context)


MESH = pl.DeviceIdType.MESH
CHUNKS = 8
DEPTH = 4
DOWN_DEPTH = 4
LAG = 2


def fused_kernel(
    n_expert,
    lengths_ref,
    own_src_ref,
    ids_ref,
    weights_ref,
    rows_ref,
    queries_ref,
    cache_hbm,
    wg_ref,
    wu_ref,
    wd_ref,
    out_ref,
    context_ref,
    rows_all,
    x32,
    xb,
    gate_buf,
    up_buf,
    down_buf,
    hid,
    y,
    sum_a,
    send_b,
    sum_b,
    y16,
    send_c,
    sum_c,
    q_all,
    src_all,
    src_smem,
    ctx_all,
    cache_ref,
    q_local,
    cache_local,
    gate_sem,
    up_sem,
    down_sem,
    row_send_z,
    row_send_2,
    row_send_1,
    row_recv,
    q_send,
    q_recv,
    src_send,
    src_recv,
    src_local,
    ctx_send,
    ctx_recv,
    a_send,
    a_recv,
    b_send,
    b_recv,
    c_send,
    c_recv,
):
    me_e = lax.axis_index("expert")
    me_r = lax.axis_index("replica")
    r2 = (me_r + 2) % 4
    r1 = me_r + 1 - 2 * (me_r % 2)
    r3 = (r1 + 2) % 4
    tokens = rows_ref.shape[0]
    local_experts, width, ff = wg_ref.shape
    experts = local_experts * n_expert
    chunk = width // CHUNKS
    band = n_expert * tokens
    requests = queries_ref.shape[0]

    def gate_copy(e):
        return pltpu.make_async_copy(
            wg_ref.at[e], gate_buf.at[e % DEPTH], gate_sem.at[e % DEPTH]
        )

    def up_copy(e):
        return pltpu.make_async_copy(wu_ref.at[e], up_buf.at[e % DEPTH], up_sem.at[e % DEPTH])

    def down_copy(c):
        return pltpu.make_async_copy(
            wd_ref.at[:, :, pl.ds(pl.multiple_of(c * chunk, 128), chunk)],
            down_buf.at[c % DOWN_DEPTH],
            down_sem.at[c % DOWN_DEPTH],
        )

    own_q = pltpu.make_async_copy(
        queries_ref,
        q_all.at[pl.ds(pl.multiple_of(me_r * requests, requests), requests)],
        q_local,
    )
    own_cache = pltpu.make_async_copy(cache_hbm, cache_ref, cache_local)
    own_q.start()
    own_cache.start()
    for e in range(DEPTH):
        gate_copy(e).start()
        up_copy(e).start()
    for c in range(DOWN_DEPTH):
        down_copy(c).start()

    mine = me_e * 4 + me_r
    lane = lax.broadcasted_iota(jnp.int32, (tokens, 128), 1)
    expert = lane % experts
    combine = jnp.zeros((tokens, 128), jnp.float32)
    for k in range(ids_ref.shape[1]):
        combine += jnp.where(ids_ref[:, k : k + 1] == expert, weights_ref[:, k : k + 1], 0.0)
    high = combine.astype(jnp.bfloat16).astype(jnp.float32)
    middle = (combine - high).astype(jnp.bfloat16).astype(jnp.float32)
    low = combine - high - middle
    pieces = jnp.where(
        lane < experts,
        high,
        jnp.where(lane < 2 * experts, middle, jnp.where(lane < 3 * experts, low, 0.0)),
    )
    rows_all[mine, :, :width] = rows_ref[...]
    rows_all[mine, :, width:] = pieces.astype(jnp.bfloat16)
    place = lax.broadcasted_iota(jnp.int32, (8, 128), 1)
    sources = jnp.zeros((8, 128), jnp.int32)
    for i in range(requests):
        sources = jnp.where(place == i, own_src_ref[i], sources)
    src_all[me_r] = sources

    barrier = pltpu.get_barrier_semaphore()
    for d in range(1, n_expert):
        pl.semaphore_signal(
            barrier, inc=1, device_id={"expert": (me_e + d) % n_expert}, device_id_type=MESH
        )
    for r in (r2, r1):
        pl.semaphore_signal(barrier, inc=1, device_id={"replica": r}, device_id_type=MESH)
    pl.semaphore_wait(barrier, n_expert + 1)

    def remote(src, dst, send, recv, **where):
        return pltpu.make_async_remote_copy(
            src_ref=src,
            dst_ref=dst,
            send_sem=send,
            recv_sem=recv,
            device_id=where,
            device_id_type=MESH,
        )

    def slot(e, r):
        return rows_all.at[e * 4 + r]

    def row_z(d):
        return remote(
            rows_all.at[mine],
            rows_all.at[mine],
            row_send_z.at[d - 1],
            row_recv.at[mine],
            expert=(me_e + d) % n_expert,
        )

    def row_to(d, r, source, sems):
        at = ((me_e + d) % n_expert) * 4 + source
        return remote(
            rows_all.at[at],
            rows_all.at[at],
            sems,
            row_recv.at[at],
            replica=r,
        )

    def arrived(at):
        return remote(
            rows_all.at[at], rows_all.at[at], row_send_z.at[0], row_recv.at[at], replica=r1
        )

    def block(ref, r):
        return ref.at[pl.ds(pl.multiple_of(r * requests, requests), requests)]

    sends = []

    def go(copy):
        copy.start()
        sends.append(copy)

    for d in range(1, n_expert):
        go(row_z(d))
    go(row_to(0, r2, me_r, row_send_2.at[0]))
    go(row_to(0, r1, me_r, row_send_1.at[0]))
    for i, r in enumerate((r2, r1)):
        go(remote(src_all.at[me_r], src_all.at[me_r], src_send.at[i], src_recv.at[me_r], replica=r))
    for d in range(1, n_expert):
        arrived(((me_e + d) % n_expert) * 4 + me_r).wait_recv()
        go(row_to(d, r2, me_r, row_send_2.at[d]))
        go(row_to(d, r1, me_r, row_send_1.at[d]))
    own_q.wait()
    for i, r in enumerate((r2, r1)):
        go(remote(block(q_all, me_r), block(q_all, me_r), q_send.at[i], q_recv.at[me_r], replica=r))
    for d in range(n_expert):
        arrived(((me_e + d) % n_expert) * 4 + r2).wait_recv()
        go(row_to(d, r1, r2, row_send_1.at[n_expert + d]))
    pltpu.make_async_copy(src_all.at[r2], src_all.at[r2], src_recv.at[r2]).wait()
    go(remote(src_all.at[r2], src_all.at[r2], src_send.at[2], src_recv.at[r2], replica=r1))
    for r in (r1, r3):
        for d in range(n_expert):
            arrived(((me_e + d) % n_expert) * 4 + r).wait_recv()

    for k, r in enumerate((me_r, r2, r1, r3)):
        for e in range(n_expert):
            x32[e * tokens : (e + 1) * tokens, :] = rows_all[e * 4 + r].astype(jnp.float32)
        xb[k * band : (k + 1) * band, :] = x32[...].astype(jnp.bfloat16)

    places = lax.broadcasted_iota(jnp.int32, (128, ff), 0)

    def first(e, carry):
        gate_copy(e).wait()
        up_copy(e).wait()
        x = xb[:, :width]
        gate = jnp.dot(x, gate_buf[e % DEPTH], preferred_element_type=jnp.float32)
        up = jnp.dot(x, up_buf[e % DEPTH], preferred_element_type=jnp.float32)
        at = me_e * local_experts + e
        hit = (places == at) | (places == at + experts) | (places == at + 2 * experts)
        weight = jnp.dot(
            xb[:, width:],
            jnp.where(hit, 1.0, 0.0).astype(jnp.bfloat16),
            preferred_element_type=jnp.float32,
        )
        hidden = (gate / (1.0 + jnp.exp(-gate)) * up).astype(jnp.bfloat16)
        hid[:, pl.ds(pl.multiple_of(e * ff, 128), ff)] = (hidden.astype(jnp.float32) * weight).astype(jnp.bfloat16)

        @pl.when(e + DEPTH < local_experts)
        def _():
            gate_copy(e + DEPTH).start()
            up_copy(e + DEPTH).start()

        return carry

    def q_forward():
        return remote(
            block(q_all, r2), block(q_all, r2), q_send.at[2], q_recv.at[r2], replica=r1
        )

    early = local_experts // 4
    late = 5 * local_experts // 8
    lax.fori_loop(0, early, first, 0)
    q_forward().wait_recv()
    go(q_forward())
    for r in (r1, r3):
        pltpu.make_async_copy(src_all.at[r], src_all.at[r], src_recv.at[r]).wait()
    local_src = pltpu.make_async_copy(src_all, src_smem, src_local)
    local_src.start()
    lax.fori_loop(early, late, first, 0)
    local_src.wait()
    for r in (r1, r3):
        remote(block(q_all, r), block(q_all, r), q_send.at[0], q_recv.at[r], replica=r1).wait_recv()

    own_cache.wait()
    positions = cache_ref.shape[2]
    seen = lax.broadcasted_iota(jnp.int32, (queries_ref.shape[1], positions), 1)
    for j in range(requests):
        held = me_r * requests + j
        user = jnp.int32(0)
        for r in range(4):
            for i in range(requests):
                user = jnp.where(src_smem[r, 0, i] == held, r * requests + i, user)
        scores = (
            lax.dot_general(
                q_all[user],
                cache_ref[j],
                (((1,), (0,)), ((), ())),
                preferred_element_type=jnp.float32,
            )
            * score_scale
        )
        scores = jnp.where(seen < lengths_ref[j], scores, -jnp.inf)
        powers = jnp.exp(scores - jnp.max(scores, axis=1, keepdims=True))
        probs = (powers / jnp.sum(powers, axis=1, keepdims=True)).astype(jnp.bfloat16)
        ctx_all[me_r * requests + j] = lax.dot_general(
            probs,
            cache_ref[j, :LAT, :],
            (((1,), (1,)), ((), ())),
            preferred_element_type=jnp.float32,
        ).astype(jnp.bfloat16)
    for i, r in enumerate((r2, r1)):
        go(
            remote(
                block(ctx_all, me_r),
                block(ctx_all, me_r),
                ctx_send.at[i],
                ctx_recv.at[me_r],
                replica=r,
            )
        )

    lax.fori_loop(late, local_experts, first, 0)

    def a_copy(c):
        return remote(
            y.at[c, pl.ds(2 * band, 2 * band)], sum_a.at[c], a_send.at[c], a_recv.at[c], replica=r1
        )

    def b_copy(c):
        return remote(send_b.at[c], sum_b.at[c], b_send.at[c], b_recv.at[c], replica=r2)

    def c_copy(c, d):
        to = (me_e + d) % n_expert
        return remote(
            send_c.at[c, to],
            sum_c.at[c, me_e],
            c_send.at[c, d - 1],
            c_recv.at[c, me_e],
            expert=to,
        )

    def c_arrived(c, d):
        at = (me_e + d) % n_expert
        return remote(
            send_c.at[c, at], sum_c.at[c, at], c_send.at[c, d - 1], c_recv.at[c, at], expert=at
        )

    def second(step, carry):
        @pl.when(step < CHUNKS)
        def _():
            down_copy(step).wait()
            y[step] = jnp.dot(
                hid[...],
                down_buf[step % DOWN_DEPTH].reshape(local_experts * ff, chunk),
                preferred_element_type=jnp.float32,
            )
            a_copy(step).start()

            @pl.when(step + DOWN_DEPTH < CHUNKS)
            def _():
                down_copy(step + DOWN_DEPTH).start()

        @pl.when((step >= LAG) & (step < CHUNKS + LAG))
        def _():
            c = step - LAG
            a_copy(c).wait_recv()
            send_b[c] = (y[c, band : 2 * band] + sum_a[c, band:]).astype(jnp.bfloat16)
            b_copy(c).start()

        @pl.when(step >= 2 * LAG)
        def _():
            c = step - 2 * LAG
            b_copy(c).wait_recv()
            y16[...] = y[c, :band] + sum_a[c, :band] + sum_b[c].astype(jnp.float32)
            for e in range(n_expert):
                send_c[c, e] = y16[e * tokens : (e + 1) * tokens].astype(jnp.bfloat16)
            for d in range(1, n_expert):
                c_copy(c, d).start()

        return carry

    def ctx_forward():
        return remote(
            block(ctx_all, r2), block(ctx_all, r2), ctx_send.at[2], ctx_recv.at[r2], replica=r1
        )

    lax.fori_loop(0, CHUNKS - 1, second, 0)
    ctx_forward().wait_recv()
    go(ctx_forward())
    lax.fori_loop(CHUNKS - 1, CHUNKS + 2 * LAG, second, 0)

    for r in (r1, r3):
        remote(
            block(ctx_all, r), block(ctx_all, r), ctx_send.at[0], ctx_recv.at[r], replica=r1
        ).wait_recv()
    for j in range(requests):
        context_ref[j] = ctx_all[own_src_ref[j]]
    for c in range(CHUNKS):
        total = send_c[c, me_e].astype(jnp.float32)
        for d in range(1, n_expert):
            c_arrived(c, d).wait_recv()
            total += sum_c[c, (me_e + d) % n_expert].astype(jnp.float32)
        out_ref[:, c * chunk : (c + 1) * chunk] = total.astype(jnp.bfloat16)

    for copy in sends:
        copy.wait_send()

    def drain(c, carry):
        a_copy(c).wait_send()
        b_copy(c).wait_send()
        for d in range(1, n_expert):
            c_copy(c, d).wait_send()
        return carry

    lax.fori_loop(0, CHUNKS, drain, 0)


def fused(
    moe_rows,
    expert_ids,
    expert_weights,
    w_gate,
    w_up,
    w_down,
    queries,
    latent_cache,
    cache_lengths,
    move_src,
):
    n_expert = lax.axis_size("expert")
    tokens = expert_ids.shape[0]
    local_experts, width, ff = w_gate.shape
    requests, heads, channels = queries.shape
    chunk = width // CHUNKS
    band = n_expert * tokens
    n = 4 * band
    bf16, f32 = jnp.bfloat16, jnp.float32
    vmem = pl.BlockSpec(memory_space=pltpu.VMEM)
    smem = pl.BlockSpec(memory_space=pltpu.SMEM)
    hbm = pl.BlockSpec(memory_space=pl.ANY)
    dma = pltpu.SemaphoreType.DMA
    return pl.pallas_call(
        functools.partial(fused_kernel, n_expert),
        out_shape=(
            jax.ShapeDtypeStruct((tokens, width), bf16),
            jax.ShapeDtypeStruct((requests, heads, LAT), bf16),
        ),
        in_specs=[smem, smem, vmem, vmem, vmem, hbm, hbm, hbm, hbm, hbm],
        out_specs=(vmem, vmem),
        scratch_shapes=[
            pltpu.VMEM((4 * n_expert, tokens, width + 128), bf16),
            pltpu.VMEM((band, width + 128), f32),
            pltpu.VMEM((n, width + 128), bf16),
            pltpu.VMEM((DEPTH, width, ff), bf16),
            pltpu.VMEM((DEPTH, width, ff), bf16),
            pltpu.VMEM((DOWN_DEPTH, local_experts, ff, chunk), bf16),
            pltpu.VMEM((n, local_experts * ff), bf16),
            pltpu.VMEM((CHUNKS, n, chunk), f32),
            pltpu.VMEM((CHUNKS, 2 * band, chunk), f32),
            pltpu.VMEM((CHUNKS, band, chunk), bf16),
            pltpu.VMEM((CHUNKS, band, chunk), bf16),
            pltpu.VMEM((band, chunk), f32),
            pltpu.VMEM((CHUNKS, n_expert, tokens, chunk), bf16),
            pltpu.VMEM((CHUNKS, n_expert, tokens, chunk), bf16),
            pltpu.VMEM((4 * requests, heads, channels), bf16),
            pltpu.VMEM((4, 8, 128), jnp.int32),
            pltpu.SMEM((4, 8, 128), jnp.int32),
            pltpu.VMEM((4 * requests, heads, LAT), bf16),
            pltpu.VMEM((requests, channels, latent_cache.shape[1]), bf16),
            dma,
            dma,
            dma((DEPTH,)),
            dma((DEPTH,)),
            dma((DOWN_DEPTH,)),
            dma((n_expert,)),
            dma((n_expert,)),
            dma((2 * n_expert,)),
            dma((4 * n_expert,)),
            dma((3,)),
            dma((4,)),
            dma((3,)),
            dma((4,)),
            dma,
            dma((3,)),
            dma((4,)),
            dma((CHUNKS,)),
            dma((CHUNKS,)),
            dma((CHUNKS,)),
            dma((CHUNKS,)),
            dma((CHUNKS, n_expert)),
            dma((CHUNKS, n_expert)),
        ],
        compiler_params=pltpu.CompilerParams(
            collective_id=0, has_side_effects=True, vmem_limit_bytes=62 * 1024 * 1024
        ),
    )(
        cache_lengths,
        move_src,
        expert_ids,
        expert_weights,
        moe_rows,
        queries,
        jnp.swapaxes(latent_cache, 1, 2),
        w_gate,
        w_up,
        w_down,
    )


def local(*arrays):
    n_expert, n_replica = lax.axis_size("expert"), lax.axis_size("replica")
    tokens = arrays[0].shape[0]
    local_experts = arrays[3].shape[0]
    small = (
        n_replica == 4
        and n_expert * tokens == 16
        and local_experts >= DEPTH
        and local_experts % 2 == 0
        and 3 * local_experts * n_expert <= 128
    )
    return fused(*arrays) if small else by_collectives(*arrays)


def solution(mesh):
    return jax.shard_map(
        local,
        mesh=mesh,
        in_specs=(
            P(("groups", "expert", "replica"), None),
            P(("groups", "expert", "replica"), None),
            P(("groups", "expert", "replica"), None),
            P("expert", None, "replica"),
            P("expert", None, "replica"),
            P("expert", "replica", None),
            P(("groups", "expert", "replica"), None, None),
            P(("groups", "expert", "replica"), None, None),
            P(("groups", "expert", "replica")),
            P(("groups", "expert", "replica")),
        ),
        out_specs=(
            P(("groups", "expert", "replica"), None),
            P(("groups", "expert", "replica"), None, None),
        ),
        check_vma=False,
    )
```
